128 devices in a mesh: prompt: 4 (over x), sample: 32 (over z, y, core).
Axes of the slice: x: 4, y: 4, z: 4, core: 2. Of those that a mesh axis runs over, the one named last changes fastest.
Arguments:
- prompt_cache: bfloat16 [4, 4096, 1024], P('prompt', 'sample'), may hold values from -6 to 6
- queries: bfloat16 [2, 2048, 8192], P(None, ('prompt', 'sample')), may hold values from -140 to 140
- new_kv: bfloat16 [2, 2048, 1024], P(None, ('prompt', 'sample')), may hold values from -12 to 12
- residual: bfloat16 [2, 2048, 4096], P(None, ('prompt', 'sample')), may hold values from -6 to 6
- out_weight: bfloat16 [8192, 4096], P('sample'), may hold values from -0.25 to 0.25
- norm_gain: float32 [4096], replicated, may hold values from 0.1 to 1.9
- gate_up: bfloat16 [128, 4096, 1536], P(('prompt', 'sample')), may hold values from -0.09375 to 0.09375
- down_weight: bfloat16 [128, 768, 4096], P(('prompt', 'sample')), may hold values from -0.21875 to 0.21875
- expert_ids: int32 [2, 2048, 8], P(None, ('prompt', 'sample')), may hold values from 0 to 127, all different within a row; in each aligned block of 16 rows (0 to 15, 16 to 31, ..., all dimensions but the last counted through in order) at most 2 rows name the same one
- route_weights: float32 [2, 2048, 8], P(None, ('prompt', 'sample')), may hold values from 0.1 to 1
Outputs:
- layer_out: bfloat16 [2, 2048, 4096], P(None, ('prompt', 'sample'))
The draws below stay inside these ranges and needn't reach their ends.
Inputs may be any that keep to these rules, and one draw needn't show every extreme that they name: `expert_ids`: each row names 8 different experts. Within the 16 rows of one device in one step (aligned blocks along the rows of a step) no expert is named by more than 2 rows, a bound that some block reaches.
All inputs are finite; a program needn't handle non-finite values.
Results may differ from the reference program's by a relative error of at most 0.022.
Values may be sent and summed in bfloat16 or wider, within the bound.
No kernel may reach another device: no remote copies, remote signals or barrier semaphores. Data moves between devices by JAX's collectives and lax.ppermute only.
A program may use at most 128 MiB of HBM per device.

```python
import math
import jax
import jax.numpy as jnp
import numpy as np
from jax import lax

D = 4096
QH = 64
KVH = 4
HD = 128
TOPK = 8
EFF = 768
STEPS = 2
ROWS = 16
PLEN = 4096
PROMPTS = 4
ROWS_ALL = 2048
EXPERTS = 128
CAP = 2


def cache_parts(key):
    first_key, second_key = jax.random.split(jax.random.fold_in(key, 40))
    key_part = jax.random.truncated_normal(first_key, -6.0, 6.0, (PROMPTS, PLEN, KVH * HD), jnp.float32)
    value_part = jax.random.truncated_normal(second_key, -6.0, 6.0, (PROMPTS, PLEN, KVH * HD), jnp.float32)
    period = min(512, PLEN // 2)
    paired = jnp.arange(PLEN) % period == period // 2 + 1
    key_part = jnp.where(paired[None, :, None], key_part, key_part)
    return (key_part, value_part)


def draw_prompt_cache(key, part):
    key_part, value_part = cache_parts(key)
    return jnp.concatenate([key_part, value_part], axis=-1).astype(jnp.bfloat16)


def draw_queries(key, part):
    own_key = jax.random.fold_in(key, 2)
    drawn = 2.5 * jax.random.truncated_normal(own_key, -6.0, 6.0, (STEPS, ROWS_ALL, QH * HD), jnp.float32)
    return drawn.astype(jnp.bfloat16)


def level_of(stream_key, dims, pieces, smallest, top_value):
    loudness, own = 1.0, jax.random.fold_in(stream_key, 6)
    for dim, shards_of in pieces:
        heights = jnp.exp(jax.random.uniform(jax.random.fold_in(own, dim), (shards_of,), jnp.float32, smallest / len(pieces), top_value / len(pieces)))
        loudness = loudness * jnp.repeat(heights, dims[dim] // shards_of).reshape([-1 if axis == dim else 1 for axis in range(len(dims))])
    return loudness


def assign_block(rng, own, number, rows, amount, top, most, lean):
    ranking = jax.random.permutation(rng, amount)
    packed, common = portions_of(amount, rows * top, most, lean, True), portions_of(amount, rows * top, most, lean, False)
    places = jnp.arange(amount)

    def named(lengths, rotation):
        used = int((lengths > 0).sum())
        fixed = max(1, used // 4)
        shifted = fixed + (places - fixed + rotation * (used - fixed)) % max(1, amount - fixed)
        return jnp.zeros((amount,), jnp.int32).at[ranking[jnp.where(places < fixed, places, shifted)]].set(jnp.asarray(lengths, jnp.int32))

    lengths = jnp.where(number % 4 == 0, named(packed, number // 4), named(common, number - number // 4 - 1))
    mixed = jax.random.permutation(jax.random.fold_in(own, 3), amount)
    source_of, taker = mixed[0:amount // 2 * 2:2], mixed[1:amount // 2 * 2:2]
    room = jnp.minimum(lengths[source_of] - 1, most - lengths[taker]) // 2
    room = jnp.where((source_of == ranking[0]) | (taker == ranking[0]) | (lengths[taker] == 0), 0, jnp.maximum(room, 0))
    shifted = jax.random.randint(jax.random.fold_in(own, 4), (amount // 2,), 0, 1 << 20) % (room + 1)
    lengths = lengths.at[source_of].add(-shifted).at[taker].add(shifted)
    items = jnp.searchsorted(jnp.cumsum(lengths), jnp.arange(rows * top), side="right").astype(jnp.int32)
    grid = items.reshape(top, rows).T
    grid = grid[jax.random.permutation(jax.random.fold_in(own, 1), rows)]
    rotation = jax.random.randint(jax.random.fold_in(own, 2), (rows, 1), 0, top)
    return jnp.take_along_axis(grid, (jnp.arange(top)[None, :] + rotation) % top, axis=1)


def portions_of(amount, total, bound, skew, full):
    loads = [(1 << 20) // math.isqrt(grade ** skew) + 1 for grade in range(1, amount + 1)]
    largest = bound if full else min(bound, max(-(-total // amount), total * loads[0] // sum(loads)))
    least = 1 if total - largest >= amount - 1 else 0
    given, surplus = [largest] + [least] * (amount - 1), total - largest - least * (amount - 1)
    while surplus > 0:
        free = [i for i in range(1, amount) if given[i] < largest] or [i for i in range(1, amount) if given[i] < bound]
        whole, remaining = sum([loads[i] for i in free]), surplus
        for i in free:
            more = min(bound - given[i], max(1, remaining * loads[i] // whole), surplus)
            given[i] = given[i] + more
            surplus = surplus - more
    return np.array(given)


def bell_draw(rng, extent, width, bound, cuts=(), kind=jnp.bfloat16):
    entries = width * jax.random.normal(rng, extent, jnp.float32)
    if cuts:
        entries = entries * level_of(rng, extent, cuts, -0.22, 0.18)
    return jnp.clip(entries, -bound, bound).astype(kind)


def setup_inputs(seed: int = 0) -> dict:
    arg_keys = jax.random.split(jax.random.key(seed), 11)
    prompt_cache = draw_prompt_cache(jax.random.fold_in(arg_keys[10], 71), 0)
    queries = draw_queries(jax.random.fold_in(arg_keys[10], 71), 0)
    new_kv = bell_draw(arg_keys[2], (STEPS, ROWS_ALL, 2 * KVH * HD), 2.0, 12.0, ((1, 128),))
    residual = bell_draw(arg_keys[3], (STEPS, ROWS_ALL, D), 1.0, 6.0, ((1, 128),))
    out_weight = bell_draw(arg_keys[4], (QH * HD, D), (KVH * HD) ** -0.5, 0.25, ((0, 32),))
    norm_gain = jnp.clip(1.0 + 0.18 * jax.random.normal(arg_keys[5], (D,), jnp.float32), 0.1, 1.9)
    gate_up = bell_draw(arg_keys[6], (EXPERTS, D, 2 * EFF), D ** -0.5, 0.09375, ((0, 128),))
    down_weight = bell_draw(arg_keys[7], (EXPERTS, EFF, D), EFF ** -0.5, 0.21875, ((0, 128),))
    expert_ids_keys = jax.random.split(jax.random.fold_in(arg_keys[8], 1), STEPS * ROWS_ALL // ROWS)
    expert_ids_turns = jax.random.permutation(jax.random.fold_in(arg_keys[8], 3), STEPS * ROWS_ALL // ROWS)
    expert_ids = jax.vmap(lambda own, number: assign_block(jax.random.fold_in(arg_keys[8], 2), own, number, ROWS, EXPERTS, TOPK, CAP, 2))(expert_ids_keys, expert_ids_turns).reshape((STEPS, ROWS_ALL, TOPK))
    route_weights = jnp.clip(jnp.exp(math.log(1.0) - 2.3025851 * jax.random.uniform(arg_keys[9], (STEPS, ROWS_ALL, TOPK), jnp.float32) ** level_of(arg_keys[9], (STEPS, ROWS_ALL, TOPK), ((1, 128),), -0.2, 0.2)), 0.1, 1.0)
    return {"prompt_cache": prompt_cache, "queries": queries, "new_kv": new_kv, "residual": residual, "out_weight": out_weight, "norm_gain": norm_gain, "gate_up": gate_up, "down_weight": down_weight, "expert_ids": expert_ids, "route_weights": route_weights}


EPSILON = 1e-06
NEG_LARGE = -1e+30
PRECISE = lax.Precision.HIGHEST

def widen(values):
    return values.astype(jnp.float32)

def attention_step(query_step, new_kv, prompt_cache, step_index):
    group_size = QH // KVH
    per_prompt = ROWS_ALL // PROMPTS
    score_scale = HD ** (-0.5)
    query_all = widen(query_step).reshape(PROMPTS, per_prompt, KVH, group_size, HD).transpose(0, 2, 1, 3, 4).reshape(PROMPTS * KVH, per_prompt, group_size, HD)
    cache_all = widen(prompt_cache).reshape(PROMPTS, PLEN, 2, KVH, HD).transpose(0, 3, 2, 1, 4).reshape(PROMPTS * KVH, 2, PLEN, HD)
    fresh_all = widen(new_kv).reshape(STEPS, PROMPTS, per_prompt, 2, KVH, HD).transpose(1, 4, 3, 0, 2, 5).reshape(PROMPTS * KVH, 2, STEPS, per_prompt, HD)
    visible = jnp.arange(STEPS) <= step_index

    def one_head(operands):
        query_block, cache_block, fresh_block = operands
        scores = jnp.dot(query_block.reshape(per_prompt * group_size, HD), cache_block[0].T, precision=PRECISE).reshape(per_prompt, group_size, PLEN) * score_scale
        fresh_scores = jnp.einsum('rgd,trd->rgt', query_block, fresh_block[0], precision=PRECISE) * score_scale
        fresh_scores = jnp.where(visible, fresh_scores, NEG_LARGE)
        largest = jnp.maximum(lax.optimization_barrier(jnp.max(scores, axis=-1)), lax.optimization_barrier(jnp.max(fresh_scores, axis=-1)))
        weights = jnp.exp(scores - largest[..., None])
        fresh_weights = jnp.where(visible, jnp.exp(fresh_scores - largest[..., None]), 0.0)
        row_total = lax.optimization_barrier(jnp.sum(weights, axis=-1)) + lax.optimization_barrier(jnp.sum(fresh_weights, axis=-1))
        rounded = widen(lax.optimization_barrier(weights.astype(jnp.bfloat16)))
        fresh_rounded = widen(lax.optimization_barrier(fresh_weights.astype(jnp.bfloat16)))
        summed = jnp.dot(rounded.reshape(per_prompt * group_size, PLEN), cache_block[1], precision=PRECISE).reshape(per_prompt, group_size, HD)
        summed = summed + jnp.einsum('rgt,trd->rgd', fresh_rounded, fresh_block[1], precision=PRECISE)
        return (summed / row_total[..., None]).astype(jnp.bfloat16)
    heads_out = lax.map(one_head, (query_all, cache_all, fresh_all))
    return heads_out.reshape(PROMPTS, KVH, per_prompt, group_size, HD).transpose(0, 2, 1, 3, 4).reshape(ROWS_ALL, QH * HD)

def expert_step(normed, expert_ids, route_weights, gate_up, down_weight):
    devices = ROWS_ALL // ROWS
    onehot = (expert_ids[..., None] == jnp.arange(EXPERTS, dtype=jnp.int32)).astype(jnp.int32)
    blocked = onehot.reshape(devices, ROWS * TOPK, EXPERTS)
    ranked = lax.optimization_barrier(jnp.sum((jnp.cumsum(blocked, axis=1) - blocked) * blocked, axis=-1)).reshape(ROWS_ALL, TOPK)
    source = jnp.arange(ROWS_ALL, dtype=jnp.int32) // ROWS
    position = source[:, None] * CAP + ranked
    row_index = jnp.broadcast_to(jnp.arange(ROWS_ALL, dtype=jnp.int32)[:, None], (ROWS_ALL, TOPK))
    slot_table = jnp.zeros((EXPERTS, devices * CAP), jnp.int32).at[expert_ids, position].set(row_index)
    normed_kept = lax.optimization_barrier(normed)

    def one_expert(operands):
        row_picks, weight_in, weight_out = operands
        inputs = widen(normed_kept[row_picks])
        projected = jnp.dot(inputs, widen(weight_in), precision=PRECISE)
        active = (jax.nn.silu(projected[:, :EFF]) * projected[:, EFF:]).astype(jnp.bfloat16)
        active = widen(lax.optimization_barrier(active))
        return jnp.dot(active, widen(weight_out), precision=PRECISE).astype(jnp.bfloat16)
    produced = lax.optimization_barrier(lax.map(one_expert, (slot_table, gate_up, down_weight)))
    picked = widen(produced[expert_ids, position])
    return lax.optimization_barrier(jnp.sum(picked * route_weights[..., None], axis=1))

def reference(prompt_cache, queries, new_kv, residual, out_weight, norm_gain, gate_up, down_weight, expert_ids, route_weights):
    results = []
    for step_number in range(STEPS):
        attended = attention_step(queries[step_number], new_kv, prompt_cache, step_number)
        attended = lax.optimization_barrier(attended)
        projected = jnp.dot(widen(attended), widen(out_weight), precision=PRECISE)
        hidden = widen(residual[step_number]) + projected
        moment = lax.optimization_barrier(jnp.mean(hidden * hidden, axis=-1, keepdims=True))
        normed = (hidden * lax.rsqrt(moment + EPSILON) * norm_gain).astype(jnp.bfloat16)
        mixture = expert_step(normed, expert_ids[step_number], route_weights[step_number], gate_up, down_weight)
        results.append((hidden + mixture).astype(jnp.bfloat16))
    return jnp.stack(results)
```

```python
import functools
import math

import jax
import jax.numpy as jnp
from jax import lax
from jax.experimental import pallas as pl
from jax.experimental.pallas import tpu as pltpu
from jax.sharding import PartitionSpec as P

QH = 64
KVH = 4
HD = 128
EPSILON = 1e-06
NEG_LARGE = -1e30
RING = 4
EXP2_SCALE = HD ** (-0.5) * math.log2(math.e)
BF = jnp.bfloat16
F32 = jnp.float32
CUT = 1024


def place():
    index = lax.axis_index("sample")
    return index // 8, (index // 2) % RING, index % 2


def along(axis, shift):
    pairs = []
    for index in range(2 * RING * RING):
        z, y, core = index // 8, (index // 2) % RING, index % 2
        if axis == "z":
            z = (z + shift) % RING
        elif axis == "y":
            y = (y + shift) % RING
        else:
            core = 1 - core
        pairs.append((index, (z * RING + y) * 2 + core))
    return pairs


def shift_to(values, axis, shift=1):
    return lax.ppermute(values, "sample", along(axis, shift))


def ring_sum(chunk, axis):
    ahead2 = chunk(2)
    half = ahead2.shape[0] // 2
    first2, second2 = ahead2[:half].astype(BF), ahead2[half:].astype(BF)
    from_behind = shift_to(first2, axis, 1)
    from_ahead = shift_to(second2, axis, -1)
    ahead1 = chunk(1)
    behind1 = chunk(3)
    got_b = shift_to(ahead1[half:].astype(BF), axis, 1)
    got_c = shift_to(behind1[:half].astype(BF), axis, -1)
    got_a = shift_to((ahead1[:half].astype(F32) + from_behind.astype(F32)).astype(BF), axis, 1)
    got_d = shift_to((behind1[half:].astype(F32) + from_ahead.astype(F32)).astype(BF), axis, -1)
    own = chunk(0).astype(F32)
    return jnp.concatenate(
        [
            own[:half] + got_a.astype(F32) + got_c.astype(F32),
            own[half:] + got_b.astype(F32) + got_d.astype(F32),
        ],
        axis=0,
    )


def attend_kernel(core_ref, own_ref, other_ref, out_ref, score_ref, *, sources, block):
    tile = pl.program_id(0)
    core = core_ref[0]
    rows = sources * 32
    here = pl.ds(tile * sources, sources)
    query = own_ref[here, 0:32, :].reshape(rows, 2 * HD)
    query = jnp.concatenate([query[:, :HD], query[:, HD:]], axis=0)
    wide = query.reshape(2, sources, 2, 16, HD).astype(F32)
    fresh_a = own_ref[here, 32:48, :].astype(F32)
    fresh_b = other_ref[here, 0:16, :].astype(F32)
    step = lax.broadcasted_iota(jnp.int32, (2, sources, 2, 16, 1), 2)
    seen_a, seen_b = core <= step, (1 - core) <= step
    score_a = jnp.sum(wide * fresh_a[None, :, None, :, :HD], axis=-1, keepdims=True)
    score_b = jnp.sum(wide * fresh_b[None, :, None, :, :HD], axis=-1, keepdims=True)
    score_a = jnp.where(seen_a, score_a, NEG_LARGE)
    score_b = jnp.where(seen_b, score_b, NEG_LARGE)
    per = block // 64
    blocks = []
    for ref, offset in ((own_ref, 48), (other_ref, 16)):
        for first in range(0, 32, per):
            blocks.append((ref, offset, first))
    largest = jnp.full((2 * rows, HD), NEG_LARGE, F32)
    for number, (ref, offset, first) in enumerate(blocks):
        keys = ref[first : first + per, offset : offset + 64, 0:HD].reshape(block, HD)
        scores = lax.dot_general(
            query, keys, (((1,), (1,)), ((), ())), preferred_element_type=F32
        )
        score_ref[:, number * block : (number + 1) * block] = scores
        for lane in range(0, block, HD):
            largest = jnp.maximum(largest, scores[:, lane : lane + HD])
    largest = jnp.maximum(
        jnp.max(largest, axis=-1, keepdims=True),
        jnp.maximum(score_a, score_b).reshape(2 * rows, 1),
    )
    summed = jnp.zeros((2 * rows, HD), F32)
    total = jnp.zeros((2 * rows, HD), F32)
    for number, (ref, offset, first) in enumerate(blocks):
        values = ref[first : first + per, offset : offset + 64, HD : 2 * HD].reshape(block, HD)
        weights = jnp.exp2(
            (score_ref[:, number * block : (number + 1) * block] - largest) * EXP2_SCALE
        )
        for lane in range(0, block, HD):
            total = total + weights[:, lane : lane + HD]
        summed = summed + jnp.dot(weights.astype(BF), values, preferred_element_type=F32)
    top = largest.reshape(2, sources, 2, 16, 1)
    weight_a = jnp.where(seen_a, jnp.exp2((score_a - top) * EXP2_SCALE), 0.0)
    weight_b = jnp.where(seen_b, jnp.exp2((score_b - top) * EXP2_SCALE), 0.0)
    row_total = jnp.sum(total, axis=-1, keepdims=True) + (weight_a + weight_b).reshape(2 * rows, 1)
    fresh = (
        weight_a.astype(BF).astype(F32) * fresh_a[None, :, None, :, HD:]
        + weight_b.astype(BF).astype(F32) * fresh_b[None, :, None, :, HD:]
    )
    attended = ((summed + fresh.reshape(2 * rows, HD)) / row_total).astype(BF)
    out_ref[:, 0:HD] = attended[:rows]
    out_ref[:, HD : 2 * HD] = attended[rows:]


def attend(core, own, other):
    sources, block = 8, 512
    return pl.pallas_call(
        functools.partial(attend_kernel, sources=sources, block=block),
        out_shape=jax.ShapeDtypeStruct((1024, 2 * HD), BF),
        grid=(32 // sources,),
        in_specs=[
            pl.BlockSpec(memory_space=pltpu.SMEM),
            pl.BlockSpec((32, 112, 256), lambda i: (0, 0, 0)),
            pl.BlockSpec((32, 80, 256), lambda i: (0, 0, 0)),
        ],
        out_specs=pl.BlockSpec((sources * 32, 2 * HD), lambda i: (i, 0)),
        scratch_shapes=[pltpu.VMEM((sources * 64, 4096), F32)],
        compiler_params=pltpu.CompilerParams(vmem_limit_bytes=40 * 2**20),
        cost_estimate=pl.CostEstimate(
            flops=4 * 2048 * 4096 * HD, bytes_accessed=4 * 2**20, transcendentals=2048 * 4096
        ),
        name="attend",
    )(core, own, other)


def expert_kernel(in_ref, gate_ref, up_ref, down_ref, out_ref, x_ref, act_ref, y_ref, *, parts):
    number = pl.program_id(0)
    near = lax.broadcasted_iota(jnp.int32, (128, 128), 0)
    far = lax.broadcasted_iota(jnp.int32, (128, 128), 1)

    @pl.when(number == 0)
    def _():
        wanted = (near % 32) // 4 * 16 + near // 32 * 4 + near % 4
        order = (wanted == far).astype(BF)
        for group in range(16):
            mixed = jnp.dot(
                order, in_ref[group * 128 : (group + 1) * 128, :], preferred_element_type=F32
            ).astype(BF)
            for cut in range(4):
                x_ref[group * 32 : (group + 1) * 32, cut * CUT : (cut + 1) * CUT] = mixed[
                    cut * 32 : (cut + 1) * 32
                ]

    width = gate_ref.shape[1]
    for part in range(parts):

        @pl.when(number == part)
        def _(part=part):
            gate = jnp.dot(x_ref[...], gate_ref[...], preferred_element_type=F32)
            up = jnp.dot(x_ref[...], up_ref[...], preferred_element_type=F32)
            act_ref[:, part * width : (part + 1) * width] = (
                gate / (1.0 + jnp.exp(-gate)) * up
            ).astype(BF)

    for cut in range(4):

        @pl.when(number == parts + cut)
        def _(cut=cut):
            y = jnp.dot(act_ref[...], down_ref[...], preferred_element_type=F32).astype(BF)
            y_ref[cut] = y

    @pl.when(number == parts + 3)
    def _():
        wanted = (near % 16) // 4 * 32 + near // 16 * 4 + near % 4
        order = (wanted == far).astype(BF)
        for group in range(16):
            together = y_ref[:, group * 32 : (group + 1) * 32, :].reshape(128, CUT)
            out_ref[group * 128 : (group + 1) * 128, :] = jnp.dot(
                order, together, preferred_element_type=F32
            ).astype(BF)


def run_expert(arrived, gate_up, down_weight):
    parts = 3
    width = gate_up.shape[1] // 2 // parts
    clamp = parts - 1
    return pl.pallas_call(
        functools.partial(expert_kernel, parts=parts),
        out_shape=jax.ShapeDtypeStruct(arrived.shape, BF),
        grid=(parts + 4,),
        in_specs=[
            pl.BlockSpec((2048, CUT), lambda i: (0, 0)),
            pl.BlockSpec((4096, width), lambda i: (0, jnp.minimum(i, clamp))),
            pl.BlockSpec((4096, width), lambda i: (0, parts + jnp.minimum(i, clamp))),
            pl.BlockSpec((768, CUT), lambda i: (0, jnp.maximum(i - parts, 0))),
        ],
        out_specs=pl.BlockSpec((2048, CUT), lambda i: (0, 0)),
        scratch_shapes=[
            pltpu.VMEM((512, 4096), BF),
            pltpu.VMEM((512, 768), BF),
            pltpu.VMEM((4, 512, CUT), BF),
        ],
        compiler_params=pltpu.CompilerParams(vmem_limit_bytes=52 * 2**20),
        cost_estimate=pl.CostEstimate(
            flops=2 * 512 * 4096 * 768 * 3, bytes_accessed=27 * 2**20, transcendentals=512 * 768
        ),
        name="expert",
    )(arrived, gate_up, gate_up, down_weight)


def on_device(
    prompt_cache,
    queries,
    new_kv,
    residual,
    out_weight,
    norm_gain,
    gate_up,
    down_weight,
    expert_ids,
    route_weights,
):
    z, y, core = place()
    rows = 32
    to_heads = queries.reshape(rows, 32, 2 * HD).transpose(1, 0, 2)
    fresh = new_kv.reshape(2, 16, 2, KVH, HD).transpose(3, 0, 1, 2, 4).reshape(KVH, 2, 16, 2 * HD)
    cached = prompt_cache.reshape(2, 64, 2, KVH, HD).transpose(3, 0, 1, 2, 4)
    cached = cached.reshape(KVH, 2, 64, 2 * HD)
    both = jnp.concatenate([fresh, cached], axis=2)
    both = jnp.broadcast_to(both[:, None], (KVH, RING, 2, 80, 2 * HD)).reshape(32, 80, 2 * HD)
    sent = jnp.concatenate([to_heads, both], axis=1)
    own = lax.all_to_all(sent, "sample", split_axis=0, concat_axis=0, tiled=True)
    other = shift_to(own[:, 32:, :], "core")
    attended = attend(core.reshape(1).astype(jnp.int32), own, other)

    halves = out_weight.reshape(2 * HD, 2, 2 * CUT)
    mine = lax.dynamic_index_in_dim(halves, core, 1, keepdims=False)
    theirs = lax.dynamic_index_in_dim(halves, 1 - core, 1, keepdims=False)
    weight = jnp.concatenate([mine, shift_to(theirs, "core")], axis=0)
    features = jnp.concatenate([attended, shift_to(attended, "core")], axis=1)
    features = features.reshape(RING, RING, 64, 4 * HD)

    def part_for(column, axis, position):
        def chunk(k):
            picked = lax.dynamic_index_in_dim(
                features, (position + k) % RING, axis, keepdims=False
            ).reshape(256, 4 * HD)
            return jnp.dot(
                picked,
                weight[:, column * CUT : (column + 1) * CUT],
                preferred_element_type=F32,
            ).astype(BF)

        return chunk

    def piece_of(values, position):
        values = values.astype(BF).reshape(RING, 64, CUT)

        def chunk(k):
            return lax.dynamic_index_in_dim(values, (position + k) % RING, 0, keepdims=False)

        return chunk

    first = ring_sum(part_for(0, 1, y), "y")
    second = ring_sum(part_for(1, 0, z), "z")
    first = ring_sum(piece_of(first, z), "z")
    second = ring_sum(piece_of(second, y), "y")
    summed = jnp.stack([first, second]).reshape(2, 2, rows, CUT)
    kept = lax.dynamic_index_in_dim(summed, core, 1, keepdims=False)
    given = lax.dynamic_index_in_dim(summed, 1 - core, 1, keepdims=False)
    got = shift_to(given.astype(BF), "core").astype(F32)
    low = jnp.where(core == 0, kept, got)
    high = jnp.where(core == 0, got, kept)
    quarters = residual.reshape(rows, 4, CUT).transpose(1, 0, 2).astype(F32)
    hidden = quarters + jnp.concatenate([low, high], axis=0)

    moment = jnp.sum(hidden * hidden, axis=(0, 2), keepdims=True) / (4 * CUT)
    normed = (hidden * lax.rsqrt(moment + EPSILON) * norm_gain.reshape(4, 1, CUT)).astype(BF)

    ids = expert_ids.reshape(2, 128)
    row_of = jnp.arange(128, dtype=jnp.int32) // 8
    same = (ids[:, :, None] == ids[:, None, :]) & (row_of[None, :] < row_of[:, None])[None]
    rank = jnp.sum(same.astype(jnp.int32), axis=-1)
    slots = (ids * 4 + jnp.arange(2, dtype=jnp.int32)[:, None] * 2 + rank).reshape(rows, 8)
    hit = slots[:, :, None] == jnp.arange(512, dtype=jnp.int32)
    route = jnp.sum(
        jnp.where(hit, route_weights.reshape(rows, 8, 1), 0.0), axis=1
    )
    chosen = jnp.any(hit, axis=1)
    eye = jnp.eye(4, dtype=bool)
    spread = chosen.T.reshape(128, 1, 4, 1, rows) & eye[None, :, None, :, None]
    spread = spread.astype(BF).reshape(2048, 4 * rows)
    outgoing = jnp.dot(spread, normed.reshape(4 * rows, CUT), preferred_element_type=F32).astype(BF)
    arrived = lax.all_to_all(
        outgoing.reshape(128, 16, CUT), ("prompt", "sample"), split_axis=0, concat_axis=0, tiled=True
    )
    produced = run_expert(arrived.reshape(2048, CUT), gate_up[0], down_weight[0])
    returned = lax.all_to_all(
        produced.reshape(128, 16, CUT), ("prompt", "sample"), split_axis=0, concat_axis=0, tiled=True
    )
    gather = jnp.where(
        eye[:, None, None, :, None], route.reshape(1, rows, 128, 1, 4), 0.0
    ).reshape(4 * rows, 2048)
    coarse = gather.astype(BF)
    fine = (gather - coarse.astype(F32)).astype(BF)
    mixture = jnp.dot(
        jnp.concatenate([coarse, fine], axis=0),
        returned.reshape(2048, CUT),
        preferred_element_type=F32,
    ).reshape(2, 4, rows, CUT)
    total = (hidden + mixture[0] + mixture[1]).astype(BF)
    return total.transpose(1, 0, 2).reshape(2, 16, 4 * CUT)


def solution(mesh):
    in_specs = (
        P("prompt", "sample", None),
        P(None, ("prompt", "sample"), None),
        P(None, ("prompt", "sample"), None),
        P(None, ("prompt", "sample"), None),
        P("sample", None),
        P(),
        P(("prompt", "sample"), None, None),
        P(("prompt", "sample"), None, None),
        P(None, ("prompt", "sample"), None),
        P(None, ("prompt", "sample"), None),
    )
    out_specs = P(None, ("prompt", "sample"), None)
    return jax.shard_map(
        on_device, mesh=mesh, in_specs=in_specs, out_specs=out_specs, check_vma=False
    )
```

```python
import functools
import math

import jax
import jax.numpy as jnp
from jax import lax
from jax.experimental import pallas as pl
from jax.experimental.pallas import tpu as pltpu
from jax.sharding import PartitionSpec as P

QH = 64
KVH = 4
HD = 128
EPSILON = 1e-06
NEG_LARGE = -1e30
RING = 4
EXP2_SCALE = HD ** (-0.5) * math.log2(math.e)
BF = jnp.bfloat16
F32 = jnp.float32
EXPERT_VMEM = 44
CUT = 1024


def place():
    index = lax.axis_index("sample")
    return index // 8, (index // 2) % RING, index % 2


def move(values, axis, rule):
    pairs = []
    for index in range(2 * RING * RING):
        z, y, core = index // 8, (index // 2) % RING, index % 2
        if axis == "z":
            z = rule(z) % RING
        elif axis == "y":
            y = rule(y) % RING
        else:
            core = rule(core)
        pairs.append((index, (z * RING + y) * 2 + core))
    return lax.ppermute(values, "sample", pairs)


def shift_to(values, axis, shift=1):
    return move(values, axis, lambda at: at + shift)


def to_other_core(values):
    return move(values, "core", lambda at: 1 - at)


def ring_sums(rings):
    halves = []
    for axis, parts in rings:
        half = parts[2].shape[0] // 2
        halves.append(
            (shift_to(parts[2][:half], axis, 1), shift_to(parts[2][half:], axis, -1))
        )
    wholes = []
    for (axis, parts), (behind, ahead) in zip(rings, halves):
        half = behind.shape[0]
        up = jnp.concatenate(
            [(parts[1][:half].astype(F32) + behind.astype(F32)).astype(BF), parts[1][half:]]
        )
        down = jnp.concatenate(
            [parts[3][:half], (parts[3][half:].astype(F32) + ahead.astype(F32)).astype(BF)]
        )
        wholes.append((shift_to(up, axis, 1), shift_to(down, axis, -1)))
    return [
        parts[0].astype(F32) + up.astype(F32) + down.astype(F32)
        for (axis, parts), (up, down) in zip(rings, wholes)
    ]


def halving_sums(rings):
    given = []
    for axis, at, values in rings:
        beside = at ^ 1
        away = jnp.stack([pick(values, beside), pick(values, 3 - beside)]).astype(BF)
        given.append(move(away, axis, lambda index: index ^ 1))
    kept = []
    for (axis, at, values), got in zip(rings, given):
        far = (pick(values, 3 - at) + got[1].astype(F32)).astype(BF)
        kept.append(move(far, axis, lambda index: 3 - index))
    return [
        pick(values, at) + got[0].astype(F32) + last.astype(F32)
        for (axis, at, values), got, last in zip(rings, given, kept)
    ]


def pick(values, index):
    return lax.dynamic_index_in_dim(values, index, 0, keepdims=False)


def pack_kernel(query_ref, fresh_ref, cache_ref, out_ref):
    for z in range(RING):
        for y in range(RING):
            block = y * RING + z
            column = (z * RING + y) * 4 * HD
            out_ref[block, 0:16, :] = query_ref[0, :, column : column + 4 * HD]
            out_ref[block, 16:32, :] = query_ref[1, :, column : column + 4 * HD]
            for side in range(2):
                source = (side * KVH + z) * HD
                for step in range(2):
                    column = (2 * step + side) * HD
                    out_ref[block, 32:48, column : column + HD] = fresh_ref[
                        step, :, source : source + HD
                    ]
                    out_ref[block, 48:112, column : column + HD] = cache_ref[
                        step * 64 : (step + 1) * 64, source : source + HD
                    ]


def pack(queries, new_kv, cache):
    vmem = pl.BlockSpec(memory_space=pltpu.VMEM)
    return pl.pallas_call(
        pack_kernel,
        out_shape=jax.ShapeDtypeStruct((RING * RING, 112, 4 * HD), BF),
        in_specs=[vmem] * 3,
        out_specs=vmem,
        name="pack",
    )(queries, new_kv, cache)


def attend_kernel(
    core_ref, own_ref, other_ref, out_ref, score_ref, value_ref, *, sources, block
):
    tile = pl.program_id(0)
    core = core_ref[0]
    rows = sources * 32
    count = 4 * rows
    here = pl.ds(tile * sources, sources)
    query = own_ref[here, 0:32, :].reshape(rows, 4 * HD)
    query = jnp.concatenate([query[:, head * HD : (head + 1) * HD] for head in range(4)], axis=0)
    per = block // 64
    blocks = []
    for ref, offset in ((own_ref, 48), (other_ref, 0)):
        for column in (0, 2 * HD):
            for first in range(0, 16, per):
                blocks.append((ref, offset, first, column))

    @pl.when(tile == 0)
    def _():
        for number, (ref, offset, first, column) in enumerate(blocks):
            values = ref[first : first + per, offset : offset + 64, column + HD : column + 2 * HD]
            value_ref[:, number * block : (number + 1) * block] = values.reshape(block, HD).T

    fresh = own_ref[here, 32:48, :]
    half = sources * 16
    own_keys, own_values = [
        jnp.concatenate(
            [
                fresh[:, :, step * 2 * HD + begin : step * 2 * HD + begin + HD].reshape(half, HD)
                for step in range(2)
            ],
            axis=0,
        )
        for begin in (0, HD)
    ]
    across = (((1,), (1,)), ((), ()))
    own_scores = lax.dot_general(own_keys, query, across, preferred_element_type=F32)
    key_at = lax.broadcasted_iota(jnp.int32, (2 * half, count), 0)
    row_at = lax.broadcasted_iota(jnp.int32, (2 * half, count), 1) % rows
    same = ((key_at % half) // 16 == row_at // 32) & (key_at % 16 == row_at % 16)
    seen = same & (key_at // half <= (row_at % 32) // 16)
    own_scores = jnp.where(seen, own_scores, NEG_LARGE)

    def fold(values, how):
        return how(values.reshape(values.shape[0] // 8, 8, count), axis=0)

    largest = fold(own_scores, jnp.max)
    for number, (ref, offset, first, column) in enumerate(blocks):
        keys = ref[first : first + per, offset : offset + 64, column : column + HD]
        scores = lax.dot_general(
            keys.reshape(block, HD), query, across, preferred_element_type=F32
        )
        score_ref[number * block : (number + 1) * block, :] = scores
        largest = jnp.maximum(largest, fold(scores, jnp.max))
    largest = jnp.max(largest, axis=0, keepdims=True)
    weights = jnp.exp2((own_scores - largest) * EXP2_SCALE)
    total = fold(weights, jnp.sum)
    summed = jnp.dot(own_values.T, weights.astype(BF), preferred_element_type=F32)
    for number in range(len(blocks)):
        weights = jnp.exp2(
            (score_ref[number * block : (number + 1) * block, :] - largest) * EXP2_SCALE
        )
        total = total + fold(weights, jnp.sum)
        summed = summed + jnp.dot(
            value_ref[:, number * block : (number + 1) * block],
            weights.astype(BF),
            preferred_element_type=F32,
        )
    attended = (summed / jnp.sum(total, axis=0, keepdims=True)).astype(BF).T
    for pair in range(2):
        column = pl.multiple_of(jnp.where(core == pair, 0, 2 * HD), 2 * HD)
        out_ref[:, pl.ds(column, 2 * HD)] = jnp.concatenate(
            [
                attended[2 * pair * rows : (2 * pair + 1) * rows],
                attended[(2 * pair + 1) * rows : (2 * pair + 2) * rows],
            ],
            axis=1,
        )


def attend(core, own, other):
    sources, block = 8, 512
    return pl.pallas_call(
        functools.partial(attend_kernel, sources=sources, block=block),
        out_shape=jax.ShapeDtypeStruct((512, 4 * HD), BF),
        grid=(16 // sources,),
        in_specs=[
            pl.BlockSpec(memory_space=pltpu.SMEM),
            pl.BlockSpec((16, 112, 512), lambda i: (0, 0, 0)),
            pl.BlockSpec((16, 64, 512), lambda i: (0, 0, 0)),
        ],
        out_specs=pl.BlockSpec((sources * 32, 4 * HD), lambda i: (i, 0)),
        scratch_shapes=[pltpu.VMEM((4096, sources * 128), F32), pltpu.VMEM((HD, 4096), BF)],
        compiler_params=pltpu.CompilerParams(vmem_limit_bytes=40 * 2**20),
        cost_estimate=pl.CostEstimate(
            flops=4 * 2048 * 4096 * HD, bytes_accessed=4 * 2**20, transcendentals=2048 * 4096
        ),
        name="attend",
    )(core, own, other)


def project_kernel(place_ref, feature_ref, own_ref, other_ref, *out_refs, order):
    half = 2 * CUT
    for column, outs in ((0, out_refs[: len(order)]), (half, out_refs[len(order) :])):
        columns = slice(column, column + half)
        for k, out_ref in zip(order, outs):
            if column == 0:
                picked = feature_ref[(place_ref[1] + k) % RING]
            else:
                picked = feature_ref[:, (place_ref[0] + k) % RING]
            picked = picked.reshape(128, 4 * HD)
            out_ref[...] = (
                jnp.dot(picked[:, : 2 * HD], own_ref[:, columns], preferred_element_type=F32)
                + jnp.dot(picked[:, 2 * HD :], other_ref[:, columns], preferred_element_type=F32)
            ).astype(BF)


def project(position, features, own, other, order):
    vmem = pl.BlockSpec(memory_space=pltpu.VMEM)
    count = 2 * len(order)
    return pl.pallas_call(
        functools.partial(project_kernel, order=order),
        out_shape=[jax.ShapeDtypeStruct((128, 2 * CUT), BF)] * count,
        in_specs=[pl.BlockSpec(memory_space=pltpu.SMEM), vmem, vmem, vmem],
        out_specs=[vmem] * count,
        compiler_params=pltpu.CompilerParams(vmem_limit_bytes=24 * 2**20),
        cost_estimate=pl.CostEstimate(
            flops=2 * 128 * 512 * 2048 * count, bytes_accessed=5 * 2**20, transcendentals=0
        ),
        name="project",
    )(position, features, own, other)


def dispatch_kernel(
    residual_ref, gain_ref, slot_ref, weight_ref, *refs
):
    sums, (hidden_ref, out_ref, map_ref) = refs[0:2], refs[2:]
    square = jnp.zeros((32, 1), F32)
    for cut in range(4):
        columns = slice(cut * CUT, (cut + 1) * CUT)
        half = slice(cut % 2 * CUT, (cut % 2 + 1) * CUT)
        projected = sums[cut // 2][:, half]
        hidden = projected + residual_ref[:, :, columns].reshape(32, CUT).astype(F32)
        hidden_ref[cut * 32 : (cut + 1) * 32, :] = hidden
        square = square + jnp.sum(hidden * hidden, axis=-1, keepdims=True)
    factor = lax.rsqrt(square / (4 * CUT) + EPSILON)
    normed = jnp.concatenate(
        [
            (
                hidden_ref[cut * 32 : (cut + 1) * 32, :]
                * factor
                * gain_ref[:, cut * CUT : (cut + 1) * CUT]
            ).astype(BF)
            for cut in range(4)
        ],
        axis=0,
    )
    for first in range(0, 2048, 256):
        target = first + lax.broadcasted_iota(jnp.int32, (256, 128), 0)
        hits = jnp.zeros((256, 128), F32)
        value = jnp.zeros((256, 128), F32)
        for choice in range(8):
            hit = target == slot_ref[choice : choice + 1, :]
            hits = jnp.where(hit, 1.0, hits)
            value = jnp.where(hit, weight_ref[choice : choice + 1, :], value)
        out_ref[first : first + 256, :] = jnp.dot(
            hits.astype(BF), normed, preferred_element_type=F32
        ).astype(BF)
        value = value.T
        coarse = value.astype(BF)
        map_ref[0:128, first : first + 256] = coarse
        map_ref[128:256, first : first + 256] = (value - coarse.astype(F32)).astype(BF)


def dispatch(residual, gain, slots, weights, sums):
    vmem = pl.BlockSpec(memory_space=pltpu.VMEM)
    return pl.pallas_call(
        dispatch_kernel,
        out_shape=[
            jax.ShapeDtypeStruct((128, CUT), F32),
            jax.ShapeDtypeStruct((2048, CUT), BF),
            jax.ShapeDtypeStruct((256, 2048), BF),
        ],
        in_specs=[vmem] * 6,
        out_specs=[vmem] * 3,
        compiler_params=pltpu.CompilerParams(vmem_limit_bytes=32 * 2**20),
        cost_estimate=pl.CostEstimate(
            flops=2 * 2048 * 128 * 1024, bytes_accessed=6 * 2**20, transcendentals=32
        ),
        name="dispatch",
    )(residual, gain, slots, weights, *sums)


def combine_kernel(map_ref, returned_ref, hidden_ref, out_ref, held_ref, arrived, *, parts):
    block = 2048 // parts
    copies = []
    for part in range(parts):
        rows = pl.ds(part * block, block)
        copy = pltpu.make_async_copy(returned_ref.at[rows], held_ref.at[rows], arrived.at[part])
        copy.start()
        copies.append(copy)
    total = jnp.zeros((256, CUT), F32)
    for part, copy in enumerate(copies):
        copy.wait()
        rows = slice(part * block, (part + 1) * block)
        total = total + jnp.dot(map_ref[:, rows], held_ref[rows, :], preferred_element_type=F32)
    total = hidden_ref[...] + total[0:128] + total[128:256]
    for cut in range(4):
        out_ref[:, :, cut * CUT : (cut + 1) * CUT] = (
            total[cut * 32 : (cut + 1) * 32].astype(BF).reshape(2, 16, CUT)
        )


def combine(gather, returned, hidden):
    parts = 4
    vmem = pl.BlockSpec(memory_space=pltpu.VMEM)
    return pl.pallas_call(
        functools.partial(combine_kernel, parts=parts),
        out_shape=jax.ShapeDtypeStruct((2, 16, 4 * CUT), BF),
        in_specs=[vmem, pl.BlockSpec(memory_space=pltpu.HBM), vmem],
        out_specs=vmem,
        scratch_shapes=[pltpu.VMEM((2048, CUT), BF), pltpu.SemaphoreType.DMA((parts,))],
        compiler_params=pltpu.CompilerParams(vmem_limit_bytes=32 * 2**20),
        cost_estimate=pl.CostEstimate(
            flops=2 * 256 * 2048 * 1024, bytes_accessed=6 * 2**20, transcendentals=0
        ),
        name="combine",
    )(gather, returned, hidden)


def expert_kernel(
    in_ref, gate_up_hbm, down_hbm, out_ref, w_ref, d_ref, x_ref, act_ref, y_ref, arrived
):
    width = w_ref.shape[3]

    def weights(part):
        return [
            pltpu.make_async_copy(
                gate_up_hbm.at[:, pl.ds(side * 3 * width + part * width, width)],
                w_ref.at[part, side],
                arrived.at[part * 2 + side],
            )
            for side in range(2)
        ]

    def down(cut):
        return pltpu.make_async_copy(
            down_hbm.at[:, pl.ds(cut * CUT, CUT)], d_ref.at[cut], arrived.at[6 + cut]
        )

    coming = weights(0)
    for copy in coming:
        copy.start()
    near = lax.broadcasted_iota(jnp.int32, (128, 128), 0)
    far = lax.broadcasted_iota(jnp.int32, (128, 128), 1)
    to_rows = (near % 32 // 4 * 16 + near // 32 * 4 + near % 4 == far).astype(BF)
    to_blocks = (near % 16 // 4 * 32 + near // 16 * 4 + near % 4 == far).astype(BF)
    for group in range(16):
        mixed = jnp.dot(
            to_rows, in_ref[group * 128 : (group + 1) * 128, :], preferred_element_type=F32
        ).astype(BF)
        for cut in range(4):
            x_ref[group * 32 : (group + 1) * 32, cut * CUT : (cut + 1) * CUT] = mixed[
                cut * 32 : (cut + 1) * 32
            ]
    for part in range(3):
        for copy in coming:
            copy.wait()
        coming = weights(part + 1) if part < 2 else [down(cut) for cut in range(4)]
        for copy in coming:
            copy.start()
        for first in range(0, 512, 256):
            rows = slice(first, first + 256)
            gate = jnp.dot(x_ref[rows], w_ref[part, 0], preferred_element_type=F32)
            up = jnp.dot(x_ref[rows], w_ref[part, 1], preferred_element_type=F32)
            act_ref[rows, part * width : (part + 1) * width] = (
                gate / (1.0 + jnp.exp(-gate)) * up
            ).astype(BF)
    for copy in coming:
        copy.wait()
    for half in range(2):
        rows = slice(half * 256, (half + 1) * 256)
        for cut in range(4):
            y_ref[cut] = jnp.dot(act_ref[rows], d_ref[cut], preferred_element_type=F32).astype(BF)
        for group in range(8):
            together = y_ref[:, group * 32 : (group + 1) * 32, :].reshape(128, CUT)
            first = half * 1024 + group * 128
            out_ref[first : first + 128, :] = jnp.dot(
                to_blocks, together, preferred_element_type=F32
            ).astype(BF)


def run_expert(arrived, gate_up, down_weight):
    width = gate_up.shape[1] // 6
    hbm = pl.BlockSpec(memory_space=pltpu.HBM)
    vmem = pl.BlockSpec(memory_space=pltpu.VMEM)
    return pl.pallas_call(
        expert_kernel,
        out_shape=jax.ShapeDtypeStruct(arrived.shape, BF),
        in_specs=[vmem, hbm, hbm],
        out_specs=vmem,
        scratch_shapes=[
            pltpu.VMEM((3, 2, 4 * CUT, width), BF),
            pltpu.VMEM((4, 3 * width, CUT), BF),
            pltpu.VMEM((512, 4 * CUT), BF),
            pltpu.VMEM((512, 3 * width), BF),
            pltpu.VMEM((4, 256, CUT), BF),
            pltpu.SemaphoreType.DMA((10,)),
        ],
        compiler_params=pltpu.CompilerParams(vmem_limit_bytes=EXPERT_VMEM * 2**20),
        cost_estimate=pl.CostEstimate(
            flops=2 * 512 * 4096 * 768 * 3, bytes_accessed=27 * 2**20, transcendentals=512 * 768
        ),
        name="expert",
    )(arrived, gate_up, down_weight)


def on_device(
    prompt_cache,
    queries,
    new_kv,
    residual,
    out_weight,
    norm_gain,
    gate_up,
    down_weight,
    expert_ids,
    route_weights,
):
    z, y, core = place()
    position = jnp.stack([z, y, core]).astype(jnp.int32)
    everyone = ("sample", "prompt")
    other_weight = to_other_core(out_weight)

    ids = expert_ids.reshape(2, 128)
    ids = ids % 32 * 4 + ids // 32
    row_of = jnp.arange(128, dtype=jnp.int32) // 8
    same = (ids[:, :, None] == ids[:, None, :]) & (row_of[None, :] < row_of[:, None])[None]
    rank = jnp.sum(same.astype(jnp.int32), axis=-1)
    slots = ids * 16 + jnp.arange(2, dtype=jnp.int32)[:, None] * 2 + rank
    slots = slots.reshape(1, 32, 8) + 4 * jnp.arange(4, dtype=jnp.int32)[:, None, None]
    slots = slots.reshape(128, 8)
    weights = jnp.broadcast_to(route_weights.reshape(1, 32, 8), (4, 32, 8)).reshape(128, 8)

    sent = pack(queries, new_kv, prompt_cache[0])
    groups = [
        [2 * (z_at * RING + y_at) + which for y_at in range(RING) for z_at in range(RING)]
        for which in range(2)
    ]
    own = lax.all_to_all(
        sent, "sample", split_axis=0, concat_axis=0, tiled=True, axis_index_groups=groups
    )
    other = to_other_core(own[:, 48:, :])
    features = attend(position[2:], own, other).reshape(RING, RING, 32, 4 * HD)

    farthest = project(position, features, out_weight, other_weight, (2,))
    nearer = project(position, features, out_weight, other_weight, (1, 3, 0))
    parts_y = [nearer[2], nearer[0], farthest[0], nearer[1]]
    parts_z = [nearer[5], nearer[3], farthest[1], nearer[4]]
    sum_y, sum_z = ring_sums([("y", parts_y), ("z", parts_z)])
    sums = halving_sums(
        [
            ("z", z, sum_y.reshape(RING, 32, 2 * CUT)),
            ("y", y, sum_z.reshape(RING, 32, 2 * CUT)),
        ]
    )

    hidden, outgoing, gather = dispatch(
        residual, norm_gain.reshape(1, -1), slots.T, weights.T, sums
    )
    arrived = lax.all_to_all(
        outgoing.reshape(128, 16, CUT), everyone, split_axis=0, concat_axis=0, tiled=True
    )
    produced = run_expert(arrived.reshape(2048, CUT), gate_up[0], down_weight[0])
    returned = lax.all_to_all(
        produced.reshape(128, 16, CUT), everyone, split_axis=0, concat_axis=0, tiled=True
    )
    return combine(gather, returned.reshape(2048, CUT), hidden)


def solution(mesh):
    in_specs = (
        P("prompt", "sample", None),
        P(None, ("prompt", "sample"), None),
        P(None, ("prompt", "sample"), None),
        P(None, ("prompt", "sample"), None),
        P("sample", None),
        P(),
        P(("prompt", "sample"), None, None),
        P(("prompt", "sample"), None, None),
        P(None, ("prompt", "sample"), None),
        P(None, ("prompt", "sample"), None),
    )
    out_specs = P(None, ("prompt", "sample"), None)
    return jax.shard_map(
        on_device, mesh=mesh, in_specs=in_specs, out_specs=out_specs, check_vma=False
    )
```

```python
import functools
import math

import jax
import jax.numpy as jnp
from jax import lax
from jax.experimental import pallas as pl
from jax.experimental.pallas import tpu as pltpu
from jax.sharding import PartitionSpec as P

QH = 64
KVH = 4
HD = 128
EPSILON = 1e-06
NEG_LARGE = -1e30
RING = 4
EXP2_SCALE = HD ** (-0.5) * math.log2(math.e)
BF = jnp.bfloat16
F32 = jnp.float32
EXPERT_VMEM = 44
CUT = 1024


def place():
    index = lax.axis_index("sample")
    return index // 8, (index // 2) % RING, index % 2


def move(values, axis, rule):
    pairs = []
    for index in range(2 * RING * RING):
        z, y, core = index // 8, (index // 2) % RING, index % 2
        if axis == "z":
            z = rule(z) % RING
        elif axis == "y":
            y = rule(y) % RING
        else:
            core = rule(core)
        pairs.append((index, (z * RING + y) * 2 + core))
    return lax.ppermute(values, "sample", pairs)


def shift_to(values, axis, shift=1):
    return move(values, axis, lambda at: at + shift)


def to_other_core(values):
    return move(values, "core", lambda at: 1 - at)


def ring_sums(rings):
    wholes = []
    for axis, parts, (behind, ahead) in rings:
        half = behind.shape[0]
        up = jnp.concatenate(
            [(parts[1][:half].astype(F32) + behind.astype(F32)).astype(BF), parts[1][half:]]
        )
        down = jnp.concatenate(
            [parts[2][:half], (parts[2][half:].astype(F32) + ahead.astype(F32)).astype(BF)]
        )
        wholes.append((shift_to(up, axis, 1), shift_to(down, axis, -1)))
    return [
        parts[0].astype(F32) + up.astype(F32) + down.astype(F32)
        for (axis, parts, passed), (up, down) in zip(rings, wholes)
    ]


def halving_sums(rings):
    given = []
    for axis, at, values in rings:
        beside = at ^ 1
        away = jnp.stack(
            [pick(values, (beside - at) % RING), pick(values, (3 - beside - at) % RING)]
        ).astype(BF)
        given.append(move(away, axis, lambda index: index ^ 1))
    kept = []
    for (axis, at, values), got in zip(rings, given):
        far = (pick(values, (3 - 2 * at) % RING) + got[1].astype(F32)).astype(BF)
        kept.append(move(far, axis, lambda index: 3 - index))
    return [
        values[0] + got[0].astype(F32) + last.astype(F32)
        for (axis, at, values), got, last in zip(rings, given, kept)
    ]


def pick(values, index):
    return lax.dynamic_index_in_dim(values, index, 0, keepdims=False)


def pack_kernel(query_ref, fresh_ref, cache_ref, out_ref):
    for z in range(RING):
        for y in range(RING):
            block = y * RING + z
            column = (z * RING + y) * 4 * HD
            out_ref[block, 0:16, :] = query_ref[0, :, column : column + 4 * HD]
            out_ref[block, 16:32, :] = query_ref[1, :, column : column + 4 * HD]
            for side in range(2):
                source = (side * KVH + z) * HD
                for step in range(2):
                    column = (2 * step + side) * HD
                    out_ref[block, 32:48, column : column + HD] = fresh_ref[
                        step, :, source : source + HD
                    ]
                    out_ref[block, 48:112, column : column + HD] = cache_ref[
                        step * 64 : (step + 1) * 64, source : source + HD
                    ]


def pack(queries, new_kv, cache):
    vmem = pl.BlockSpec(memory_space=pltpu.VMEM)
    return pl.pallas_call(
        pack_kernel,
        out_shape=jax.ShapeDtypeStruct((RING * RING, 112, 4 * HD), BF),
        in_specs=[vmem] * 3,
        out_specs=vmem,
        name="pack",
    )(queries, new_kv, cache)


def attend_kernel(place_ref, own_ref, other_ref, *refs, offsets, block):
    out_ref, score_ref, value_ref = refs[-3:]
    core = place_ref[2]
    sources = len(offsets)
    rows = sources * 32
    count = 4 * rows
    at = [
        (place_ref[1] + dy) % RING * RING + (place_ref[0] + dz) % RING for dy, dz in offsets
    ]
    query = jnp.concatenate([own_ref[index, 0:32, :] for index in at], axis=0)
    query = jnp.concatenate([query[:, head * HD : (head + 1) * HD] for head in range(4)], axis=0)
    per = block // 64
    blocks = []
    for ref, offset in ((own_ref, 48), (other_ref, 0)):
        for column in (0, 2 * HD):
            for first in range(0, 16, per):
                blocks.append((ref, offset, first, column))
    for number, (ref, offset, first, column) in enumerate(blocks):
        values = ref[first : first + per, offset : offset + 64, column + HD : column + 2 * HD]
        value_ref[:, number * block : (number + 1) * block] = values.reshape(block, HD).T

    fresh = jnp.concatenate([own_ref[index, 32:48, :] for index in at], axis=0)
    half = sources * 16
    own_keys, own_values = [
        jnp.concatenate(
            [
                fresh[:, step * 2 * HD + begin : step * 2 * HD + begin + HD]
                for step in range(2)
            ],
            axis=0,
        )
        for begin in (0, HD)
    ]
    across = (((1,), (1,)), ((), ()))
    own_scores = lax.dot_general(own_keys, query, across, preferred_element_type=F32)
    key_at = lax.broadcasted_iota(jnp.int32, (2 * half, count), 0)
    row_at = lax.broadcasted_iota(jnp.int32, (2 * half, count), 1) % rows
    same = ((key_at % half) // 16 == row_at // 32) & (key_at % 16 == row_at % 16)
    seen = same & (key_at // half <= (row_at % 32) // 16)
    own_scores = jnp.where(seen, own_scores, NEG_LARGE)

    def fold(values, how):
        return how(values.reshape(values.shape[0] // 8, 8, count), axis=0)

    largest = fold(own_scores, jnp.max)
    for number, (ref, offset, first, column) in enumerate(blocks):
        keys = ref[first : first + per, offset : offset + 64, column : column + HD]
        scores = lax.dot_general(
            keys.reshape(block, HD), query, across, preferred_element_type=F32
        )
        score_ref[number * block : (number + 1) * block, :] = scores
        largest = jnp.maximum(largest, fold(scores, jnp.max))
    largest = jnp.max(largest, axis=0, keepdims=True)
    weights = jnp.exp2((own_scores - largest) * EXP2_SCALE)
    total = fold(weights, jnp.sum)
    summed = jnp.dot(own_values.T, weights.astype(BF), preferred_element_type=F32)
    for number in range(len(blocks)):
        weights = jnp.exp2(
            (score_ref[number * block : (number + 1) * block, :] - largest) * EXP2_SCALE
        )
        total = total + fold(weights, jnp.sum)
        summed = summed + jnp.dot(
            value_ref[:, number * block : (number + 1) * block],
            weights.astype(BF),
            preferred_element_type=F32,
        )
    attended = (summed / jnp.sum(total, axis=0, keepdims=True)).astype(BF).T
    for pair in range(2):
        column = pl.multiple_of(jnp.where(core == pair, 0, 2 * HD), 2 * HD)
        out_ref[:, pl.ds(column, 2 * HD)] = jnp.concatenate(
            [
                attended[2 * pair * rows : (2 * pair + 1) * rows],
                attended[(2 * pair + 1) * rows : (2 * pair + 2) * rows],
            ],
            axis=1,
        )


FIRST = [(2, 0), (2, 1), (2, 2), (2, 3), (0, 2), (1, 2), (3, 2), (0, 0)]
SECOND = [(dy, dz) for dy in (0, 1, 3) for dz in (0, 1, 3) if (dy, dz) != (0, 0)]


def attend(position, own, other, ready=None):
    first_call = ready is None
    offsets = FIRST if first_call else SECOND
    rows = 32 * len(offsets)
    vmem = pl.BlockSpec(memory_space=pltpu.VMEM)
    out = jax.ShapeDtypeStruct((rows, 4 * HD), BF)
    specs = [pl.BlockSpec(memory_space=pltpu.SMEM), vmem, vmem]
    return pl.pallas_call(
        functools.partial(attend_kernel, offsets=offsets, block=512),
        out_shape=out,
        in_specs=specs if first_call else specs + [vmem],
        out_specs=vmem,
        scratch_shapes=[pltpu.VMEM((4096, 4 * rows), F32), pltpu.VMEM((HD, 4096), BF)],
        compiler_params=pltpu.CompilerParams(vmem_limit_bytes=26 * 2**20),
        cost_estimate=pl.CostEstimate(
            flops=2 * 2048 * 4096 * HD, bytes_accessed=4 * 2**20, transcendentals=1024 * 4096
        ),
        name="attend_first" if first_call else "attend_second",
    )(position, own, other, *(() if first_call else (ready,)))


def rows_of(feature_refs, offset):
    which = 0 if offset in FIRST else 1
    first = 32 * (FIRST, SECOND)[which].index(offset)
    return feature_refs[which][first : first + 32, :]


def partial_sums(own_ref, other_ref, feature_refs, axis, k):
    columns = slice(axis * 2 * CUT, (axis + 1) * 2 * CUT)
    offsets = [(k, along) if axis == 0 else (along, k) for along in range(RING)]
    picked = jnp.concatenate([rows_of(feature_refs, offset) for offset in offsets], axis=0)
    return (
        jnp.dot(picked[:, : 2 * HD], own_ref[:, columns], preferred_element_type=F32)
        + jnp.dot(picked[:, 2 * HD :], other_ref[:, columns], preferred_element_type=F32)
    ).astype(BF)


def project_far_kernel(own_ref, other_ref, feature_ref, *out_refs):
    for axis in range(2):
        partial = partial_sums(own_ref, other_ref, [feature_ref], axis, 2)
        out_refs[2 * axis][...] = partial[:64]
        out_refs[2 * axis + 1][...] = partial[64:]
    out_refs[4][...] = jnp.zeros_like(out_refs[4])


def project_far(own, other, features):
    vmem = pl.BlockSpec(memory_space=pltpu.VMEM)
    return pl.pallas_call(
        project_far_kernel,
        out_shape=[jax.ShapeDtypeStruct((64, 2 * CUT), BF)] * 4
        + [jax.ShapeDtypeStruct((8, HD), F32)],
        in_specs=[vmem] * 3,
        out_specs=[vmem] * 5,
        compiler_params=pltpu.CompilerParams(vmem_limit_bytes=12 * 2**20),
        cost_estimate=pl.CostEstimate(
            flops=4 * 128 * 512 * 2048, bytes_accessed=5 * 2**20, transcendentals=0
        ),
        name="project_far",
    )(own, other, features)


def project_near_kernel(own_ref, other_ref, *refs):
    out_refs = refs[-6:]
    for axis in range(2):
        for number, k in enumerate((0, 1, 3)):
            out_refs[3 * axis + number][...] = partial_sums(
                own_ref, other_ref, refs[:2], axis, k
            )


def project_near(own, other, features, ready):
    vmem = pl.BlockSpec(memory_space=pltpu.VMEM)
    return pl.pallas_call(
        project_near_kernel,
        out_shape=[jax.ShapeDtypeStruct((128, 2 * CUT), BF)] * 6,
        in_specs=[vmem] * 4 + [pl.BlockSpec(memory_space=pl.ANY)] * len(ready),
        out_specs=[vmem] * 6,
        compiler_params=pltpu.CompilerParams(vmem_limit_bytes=12 * 2**20),
        cost_estimate=pl.CostEstimate(
            flops=12 * 128 * 512 * 2048, bytes_accessed=5 * 2**20, transcendentals=0
        ),
        name="project_near",
    )(own, other, *features, *ready)


def dispatch_kernel(
    residual_ref, gain_ref, slot_ref, weight_ref, *refs
):
    sums, (hidden_ref, out_ref, map_ref) = refs[0:2], refs[2:]
    square = jnp.zeros((32, 1), F32)
    for cut in range(4):
        columns = slice(cut * CUT, (cut + 1) * CUT)
        half = slice(cut % 2 * CUT, (cut % 2 + 1) * CUT)
        projected = sums[cut // 2][:, half]
        hidden = projected + residual_ref[:, :, columns].reshape(32, CUT).astype(F32)
        hidden_ref[cut * 32 : (cut + 1) * 32, :] = hidden
        square = square + jnp.sum(hidden * hidden, axis=-1, keepdims=True)
    factor = lax.rsqrt(square / (4 * CUT) + EPSILON)
    normed = jnp.concatenate(
        [
            (
                hidden_ref[cut * 32 : (cut + 1) * 32, :]
                * factor
                * gain_ref[:, cut * CUT : (cut + 1) * CUT]
            ).astype(BF)
            for cut in range(4)
        ],
        axis=0,
    )
    for first in range(0, 2048, 256):
        target = first + lax.broadcasted_iota(jnp.int32, (256, 128), 0)
        hits = jnp.zeros((256, 128), F32)
        value = jnp.zeros((256, 128), F32)
        for choice in range(8):
            hit = target == slot_ref[choice : choice + 1, :]
            hits = jnp.where(hit, 1.0, hits)
            value = jnp.where(hit, weight_ref[choice : choice + 1, :], value)
        out_ref[first : first + 256, :] = jnp.dot(
            hits.astype(BF), normed, preferred_element_type=F32
        ).astype(BF)
        value = value.T
        coarse = value.astype(BF)
        map_ref[0:128, first : first + 256] = coarse
        map_ref[128:256, first : first + 256] = (value - coarse.astype(F32)).astype(BF)


def dispatch(residual, gain, slots, weights, sums):
    vmem = pl.BlockSpec(memory_space=pltpu.VMEM)
    return pl.pallas_call(
        dispatch_kernel,
        out_shape=[
            jax.ShapeDtypeStruct((128, CUT), F32),
            jax.ShapeDtypeStruct((2048, CUT), BF),
            jax.ShapeDtypeStruct((256, 2048), BF),
        ],
        in_specs=[vmem] * 6,
        out_specs=[vmem] * 3,
        compiler_params=pltpu.CompilerParams(vmem_limit_bytes=32 * 2**20),
        cost_estimate=pl.CostEstimate(
            flops=2 * 2048 * 128 * 1024, bytes_accessed=6 * 2**20, transcendentals=32
        ),
        name="dispatch",
    )(residual, gain, slots, weights, *sums)


def combine_kernel(map_ref, returned_ref, hidden_ref, out_ref, held_ref, arrived, *, parts):
    block = 2048 // parts
    copies = []
    for part in range(parts):
        rows = pl.ds(part * block, block)
        copy = pltpu.make_async_copy(returned_ref.at[rows], held_ref.at[rows], arrived.at[part])
        copy.start()
        copies.append(copy)
    total = jnp.zeros((256, CUT), F32)
    for part, copy in enumerate(copies):
        copy.wait()
        rows = slice(part * block, (part + 1) * block)
        total = total + jnp.dot(map_ref[:, rows], held_ref[rows, :], preferred_element_type=F32)
    total = hidden_ref[...] + total[0:128] + total[128:256]
    for cut in range(4):
        out_ref[:, :, cut * CUT : (cut + 1) * CUT] = (
            total[cut * 32 : (cut + 1) * 32].astype(BF).reshape(2, 16, CUT)
        )


def combine(gather, returned, hidden):
    parts = 4
    vmem = pl.BlockSpec(memory_space=pltpu.VMEM)
    return pl.pallas_call(
        functools.partial(combine_kernel, parts=parts),
        out_shape=jax.ShapeDtypeStruct((2, 16, 4 * CUT), BF),
        in_specs=[vmem, pl.BlockSpec(memory_space=pltpu.HBM), vmem],
        out_specs=vmem,
        scratch_shapes=[pltpu.VMEM((2048, CUT), BF), pltpu.SemaphoreType.DMA((parts,))],
        compiler_params=pltpu.CompilerParams(vmem_limit_bytes=32 * 2**20),
        cost_estimate=pl.CostEstimate(
            flops=2 * 256 * 2048 * 1024, bytes_accessed=6 * 2**20, transcendentals=0
        ),
        name="combine",
    )(gather, returned, hidden)


def expert_kernel(
    in_ref, gate_up_hbm, down_hbm, out_ref, w_ref, d_ref, x_ref, act_ref, y_ref, arrived
):
    width = w_ref.shape[3]

    def weights(part):
        return [
            pltpu.make_async_copy(
                gate_up_hbm.at[:, pl.ds(side * 3 * width + part * width, width)],
                w_ref.at[part, side],
                arrived.at[part * 2 + side],
            )
            for side in range(2)
        ]

    def down(cut):
        return pltpu.make_async_copy(
            down_hbm.at[:, pl.ds(cut * CUT, CUT)], d_ref.at[cut], arrived.at[6 + cut]
        )

    coming = weights(0)
    for copy in coming:
        copy.start()
    near = lax.broadcasted_iota(jnp.int32, (128, 128), 0)
    far = lax.broadcasted_iota(jnp.int32, (128, 128), 1)
    to_rows = (near % 32 // 4 * 16 + near // 32 * 4 + near % 4 == far).astype(BF)
    to_blocks = (near % 16 // 4 * 32 + near // 16 * 4 + near % 4 == far).astype(BF)
    for group in range(16):
        mixed = jnp.dot(
            to_rows, in_ref[group * 128 : (group + 1) * 128, :], preferred_element_type=F32
        ).astype(BF)
        for cut in range(4):
            x_ref[group * 32 : (group + 1) * 32, cut * CUT : (cut + 1) * CUT] = mixed[
                cut * 32 : (cut + 1) * 32
            ]
    for part in range(3):
        for copy in coming:
            copy.wait()
        coming = weights(part + 1) if part < 2 else [down(cut) for cut in range(4)]
        for copy in coming:
            copy.start()
        for first in range(0, 512, 256):
            rows = slice(first, first + 256)
            gate = jnp.dot(x_ref[rows], w_ref[part, 0], preferred_element_type=F32)
            up = jnp.dot(x_ref[rows], w_ref[part, 1], preferred_element_type=F32)
            act_ref[rows, part * width : (part + 1) * width] = (
                gate / (1.0 + jnp.exp(-gate)) * up
            ).astype(BF)
    for copy in coming:
        copy.wait()
    for half in range(2):
        rows = slice(half * 256, (half + 1) * 256)
        for cut in range(4):
            y_ref[cut] = jnp.dot(act_ref[rows], d_ref[cut], preferred_element_type=F32).astype(BF)
        for group in range(8):
            together = y_ref[:, group * 32 : (group + 1) * 32, :].reshape(128, CUT)
            first = half * 1024 + group * 128
            out_ref[first : first + 128, :] = jnp.dot(
                to_blocks, together, preferred_element_type=F32
            ).astype(BF)


def run_expert(arrived, gate_up, down_weight):
    width = gate_up.shape[1] // 6
    hbm = pl.BlockSpec(memory_space=pltpu.HBM)
    vmem = pl.BlockSpec(memory_space=pltpu.VMEM)
    return pl.pallas_call(
        expert_kernel,
        out_shape=jax.ShapeDtypeStruct(arrived.shape, BF),
        in_specs=[vmem, hbm, hbm],
        out_specs=vmem,
        scratch_shapes=[
            pltpu.VMEM((3, 2, 4 * CUT, width), BF),
            pltpu.VMEM((4, 3 * width, CUT), BF),
            pltpu.VMEM((512, 4 * CUT), BF),
            pltpu.VMEM((512, 3 * width), BF),
            pltpu.VMEM((4, 256, CUT), BF),
            pltpu.SemaphoreType.DMA((10,)),
        ],
        compiler_params=pltpu.CompilerParams(vmem_limit_bytes=EXPERT_VMEM * 2**20),
        cost_estimate=pl.CostEstimate(
            flops=2 * 512 * 4096 * 768 * 3, bytes_accessed=27 * 2**20, transcendentals=512 * 768
        ),
        name="expert",
    )(arrived, gate_up, down_weight)


def on_device(
    prompt_cache,
    queries,
    new_kv,
    residual,
    out_weight,
    norm_gain,
    gate_up,
    down_weight,
    expert_ids,
    route_weights,
):
    z, y, core = place()
    position = jnp.stack([z, y, core]).astype(jnp.int32)
    everyone = ("sample", "prompt")
    other_weight = to_other_core(out_weight)

    ids = expert_ids.reshape(2, 128)
    ids = ids % 32 * 4 + ids // 32
    row_of = jnp.arange(128, dtype=jnp.int32) // 8
    same = (ids[:, :, None] == ids[:, None, :]) & (row_of[None, :] < row_of[:, None])[None]
    rank = jnp.sum(same.astype(jnp.int32), axis=-1)
    slots = ids * 16 + jnp.arange(2, dtype=jnp.int32)[:, None] * 2 + rank
    slots = slots.reshape(1, 32, 8) + 4 * jnp.arange(4, dtype=jnp.int32)[:, None, None]
    slots = slots.reshape(128, 8)
    weights = jnp.broadcast_to(route_weights.reshape(1, 32, 8), (4, 32, 8)).reshape(128, 8)

    sent = pack(queries, new_kv, prompt_cache[0])
    groups = [
        [2 * (z_at * RING + y_at) + which for y_at in range(RING) for z_at in range(RING)]
        for which in range(2)
    ]
    own = lax.all_to_all(
        sent, "sample", split_axis=0, concat_axis=0, tiled=True, axis_index_groups=groups
    )
    other = to_other_core(own[:, 48:, :])
    features = attend(position, own, other)
    *far, token = project_far(out_weight, other_weight, features)
    steps = (("y", 1), ("y", -1), ("z", 1), ("z", -1))
    passed = [shift_to(part, *step) for part, step in zip(far, steps)]
    rest = attend(position, own, other, token)
    near = project_near(out_weight, other_weight, [features, rest], passed)
    sum_y, sum_z = ring_sums([("y", near[:3], passed[:2]), ("z", near[3:], passed[2:])])
    sums = halving_sums(
        [
            ("z", z, sum_y.reshape(RING, 32, 2 * CUT)),
            ("y", y, sum_z.reshape(RING, 32, 2 * CUT)),
        ]
    )

    hidden, outgoing, gather = dispatch(
        residual, norm_gain.reshape(1, -1), slots.T, weights.T, sums
    )
    arrived = lax.all_to_all(
        outgoing.reshape(128, 16, CUT), everyone, split_axis=0, concat_axis=0, tiled=True
    )
    produced = run_expert(arrived.reshape(2048, CUT), gate_up[0], down_weight[0])
    returned = lax.all_to_all(
        produced.reshape(128, 16, CUT), everyone, split_axis=0, concat_axis=0, tiled=True
    )
    return combine(gather, returned.reshape(2048, CUT), hidden)


def solution(mesh):
    in_specs = (
        P("prompt", "sample", None),
        P(None, ("prompt", "sample"), None),
        P(None, ("prompt", "sample"), None),
        P(None, ("prompt", "sample"), None),
        P("sample", None),
        P(),
        P(("prompt", "sample"), None, None),
        P(("prompt", "sample"), None, None),
        P(None, ("prompt", "sample"), None),
        P(None, ("prompt", "sample"), None),
    )
    out_specs = P(None, ("prompt", "sample"), None)
    return jax.shard_map(
        on_device, mesh=mesh, in_specs=in_specs, out_specs=out_specs, check_vma=False
    )
```

```python
import functools
import math

import jax
import jax.numpy as jnp
from jax import lax
from jax.experimental import pallas as pl
from jax.experimental.pallas import tpu as pltpu
from jax.sharding import PartitionSpec as P

QH = 64
KVH = 4
HD = 128
EPSILON = 1e-06
NEG_LARGE = -1e30
RING = 4
EXP2_SCALE = HD ** (-0.5) * math.log2(math.e)
BF = jnp.bfloat16
F32 = jnp.float32
EXPERT_VMEM = 44
CUT = 1024


def place():
    index = lax.axis_index("sample")
    return index // 8, (index // 2) % RING, index % 2


def move(values, axis, rule):
    pairs = []
    for index in range(2 * RING * RING):
        z, y, core = index // 8, (index // 2) % RING, index % 2
        if axis == "z":
            z = rule(z) % RING
        elif axis == "y":
            y = rule(y) % RING
        else:
            core = rule(core)
        pairs.append((index, (z * RING + y) * 2 + core))
    return lax.ppermute(values, "sample", pairs)


def shift_to(values, axis, shift=1):
    return move(values, axis, lambda at: at + shift)


def to_other_core(values):
    return move(values, "core", lambda at: 1 - at)


def ring_sums(rings):
    wholes = []
    for axis, parts, (behind, ahead) in rings:
        half = behind.shape[0]
        up = jnp.concatenate(
            [(parts[1][:half].astype(F32) + behind.astype(F32)).astype(BF), parts[1][half:]]
        )
        down = jnp.concatenate(
            [parts[2][:half], (parts[2][half:].astype(F32) + ahead.astype(F32)).astype(BF)]
        )
        wholes.append((shift_to(up, axis, 1), shift_to(down, axis, -1)))
    return [
        parts[0].astype(F32) + up.astype(F32) + down.astype(F32)
        for (axis, parts, passed), (up, down) in zip(rings, wholes)
    ]


def halving_sums(rings):
    given = []
    for axis, at, values in rings:
        beside = at ^ 1
        away = jnp.stack(
            [pick(values, (beside - at) % RING), pick(values, (3 - beside - at) % RING)]
        ).astype(BF)
        given.append(move(away, axis, lambda index: index ^ 1))
    kept = []
    for (axis, at, values), got in zip(rings, given):
        far = (pick(values, (3 - 2 * at) % RING) + got[1].astype(F32)).astype(BF)
        kept.append(move(far, axis, lambda index: 3 - index))
    return [
        values[0] + got[0].astype(F32) + last.astype(F32)
        for (axis, at, values), got, last in zip(rings, given, kept)
    ]


def pick(values, index):
    return lax.dynamic_index_in_dim(values, index, 0, keepdims=False)


def pack_kernel(query_ref, fresh_ref, cache_ref, out_ref):
    for z in range(RING):
        for y in range(RING):
            block = y * RING + z
            column = (z * RING + y) * 4 * HD
            out_ref[block, 0:16, :] = query_ref[0, :, column : column + 4 * HD]
            out_ref[block, 16:32, :] = query_ref[1, :, column : column + 4 * HD]
            for side in range(2):
                source = (side * KVH + z) * HD
                for step in range(2):
                    column = (2 * step + side) * HD
                    out_ref[block, 32:48, column : column + HD] = fresh_ref[
                        step, :, source : source + HD
                    ]
                    out_ref[block, 48:112, column : column + HD] = cache_ref[
                        step * 64 : (step + 1) * 64, source : source + HD
                    ]


def pack(queries, new_kv, cache):
    vmem = pl.BlockSpec(memory_space=pltpu.VMEM)
    return pl.pallas_call(
        pack_kernel,
        out_shape=jax.ShapeDtypeStruct((RING * RING, 112, 4 * HD), BF),
        in_specs=[vmem] * 3,
        out_specs=vmem,
        name="pack",
    )(queries, new_kv, cache)


def attend_kernel(place_ref, own_ref, other_hbm, *refs, offsets, block):
    out_ref, score_ref, value_ref, other_ref, arrived = refs[-5:]
    coming = pltpu.make_async_copy(other_hbm, other_ref, arrived.at[0])
    coming.start()
    core = place_ref[2]
    sources = len(offsets)
    rows = sources * 32
    count = 4 * rows
    at = [
        (place_ref[1] + dy) % RING * RING + (place_ref[0] + dz) % RING for dy, dz in offsets
    ]
    query = jnp.concatenate([own_ref[index, 0:32, :] for index in at], axis=0)
    query = jnp.concatenate([query[:, head * HD : (head + 1) * HD] for head in range(4)], axis=0)
    per = block // 64
    blocks = []
    for ref, offset in ((own_ref, 48), (other_ref, 0)):
        for column in (0, 2 * HD):
            for first in range(0, 16, per):
                blocks.append((ref, offset, first, column))

    fresh = jnp.concatenate([own_ref[index, 32:48, :] for index in at], axis=0)
    half = sources * 16
    own_keys, own_values = [
        jnp.concatenate(
            [
                fresh[:, step * 2 * HD + begin : step * 2 * HD + begin + HD]
                for step in range(2)
            ],
            axis=0,
        )
        for begin in (0, HD)
    ]
    across = (((1,), (1,)), ((), ()))
    own_scores = lax.dot_general(own_keys, query, across, preferred_element_type=F32)
    key_at = lax.broadcasted_iota(jnp.int32, (2 * half, count), 0)
    row_at = lax.broadcasted_iota(jnp.int32, (2 * half, count), 1) % rows
    same = ((key_at % half) // 16 == row_at // 32) & (key_at % 16 == row_at % 16)
    seen = same & (key_at // half <= (row_at % 32) // 16)
    own_scores = jnp.where(seen, own_scores, NEG_LARGE)

    def fold(values, how):
        return how(values.reshape(values.shape[0] // 8, 8, count), axis=0)

    largest = fold(own_scores, jnp.max)
    for number, (ref, offset, first, column) in enumerate(blocks):
        if number == len(blocks) // 2:
            coming.wait()
        keys = ref[first : first + per, offset : offset + 64, column : column + HD]
        scores = lax.dot_general(
            keys.reshape(block, HD), query, across, preferred_element_type=F32
        )
        score_ref[number * block : (number + 1) * block, :] = scores
        largest = jnp.maximum(largest, fold(scores, jnp.max))
    for number, (ref, offset, first, column) in enumerate(blocks):
        values = ref[first : first + per, offset : offset + 64, column + HD : column + 2 * HD]
        value_ref[:, number * block : (number + 1) * block] = values.reshape(block, HD).T
    largest = jnp.max(largest, axis=0, keepdims=True)
    weights = jnp.exp2((own_scores - largest) * EXP2_SCALE)
    total = fold(weights, jnp.sum)
    summed = jnp.dot(own_values.T, weights.astype(BF), preferred_element_type=F32)
    for number in range(len(blocks)):
        weights = jnp.exp2(
            (score_ref[number * block : (number + 1) * block, :] - largest) * EXP2_SCALE
        )
        total = total + fold(weights, jnp.sum)
        summed = summed + jnp.dot(
            value_ref[:, number * block : (number + 1) * block],
            weights.astype(BF),
            preferred_element_type=F32,
        )
    attended = (summed / jnp.sum(total, axis=0, keepdims=True)).astype(BF).T
    for pair in range(2):
        column = pl.multiple_of(jnp.where(core == pair, 0, 2 * HD), 2 * HD)
        out_ref[:, pl.ds(column, 2 * HD)] = jnp.concatenate(
            [
                attended[2 * pair * rows : (2 * pair + 1) * rows],
                attended[(2 * pair + 1) * rows : (2 * pair + 2) * rows],
            ],
            axis=1,
        )


FIRST = [(2, 0), (2, 1), (2, 2), (2, 3), (0, 2), (1, 2), (3, 2), (0, 0)]
SECOND = [(dy, dz) for dy in (0, 1, 3) for dz in (0, 1, 3) if (dy, dz) != (0, 0)]


def attend(position, own, other, ready=None):
    first_call = ready is None
    offsets = FIRST if first_call else SECOND
    rows = 32 * len(offsets)
    vmem = pl.BlockSpec(memory_space=pltpu.VMEM)
    out = jax.ShapeDtypeStruct((rows, 4 * HD), BF)
    specs = [pl.BlockSpec(memory_space=pltpu.SMEM), vmem, pl.BlockSpec(memory_space=pl.ANY)]
    return pl.pallas_call(
        functools.partial(attend_kernel, offsets=offsets, block=512),
        out_shape=out,
        in_specs=specs if first_call else specs + [vmem],
        out_specs=vmem,
        scratch_shapes=[
            pltpu.VMEM((4096, 4 * rows), F32),
            pltpu.VMEM((HD, 4096), BF),
            pltpu.VMEM((16, 64, 4 * HD), BF),
            pltpu.SemaphoreType.DMA((1,)),
        ],
        compiler_params=pltpu.CompilerParams(vmem_limit_bytes=26 * 2**20),
        cost_estimate=pl.CostEstimate(
            flops=2 * 2048 * 4096 * HD, bytes_accessed=4 * 2**20, transcendentals=1024 * 4096
        ),
        name="attend_first" if first_call else "attend_second",
    )(position, own, other, *(() if first_call else (ready,)))


def rows_of(feature_refs, offset):
    which = 0 if offset in FIRST else 1
    first = 32 * (FIRST, SECOND)[which].index(offset)
    return feature_refs[which][first : first + 32, :]


def partial_sums(own_ref, other_ref, feature_refs, axis, k):
    columns = slice(axis * 2 * CUT, (axis + 1) * 2 * CUT)
    offsets = [(k, along) if axis == 0 else (along, k) for along in range(RING)]
    picked = jnp.concatenate([rows_of(feature_refs, offset) for offset in offsets], axis=0)
    return (
        jnp.dot(picked[:, : 2 * HD], own_ref[:, columns], preferred_element_type=F32)
        + jnp.dot(picked[:, 2 * HD :], other_ref[:, columns], preferred_element_type=F32)
    ).astype(BF)


def project_far_kernel(own_ref, other_ref, feature_ref, *out_refs):
    for axis in range(2):
        partial = partial_sums(own_ref, other_ref, [feature_ref], axis, 2)
        out_refs[2 * axis][...] = partial[:64]
        out_refs[2 * axis + 1][...] = partial[64:]
    out_refs[4][...] = jnp.zeros_like(out_refs[4])


def project_far(own, other, features):
    vmem = pl.BlockSpec(memory_space=pltpu.VMEM)
    return pl.pallas_call(
        project_far_kernel,
        out_shape=[jax.ShapeDtypeStruct((64, 2 * CUT), BF)] * 4
        + [jax.ShapeDtypeStruct((8, HD), F32)],
        in_specs=[vmem] * 3,
        out_specs=[vmem] * 5,
        compiler_params=pltpu.CompilerParams(vmem_limit_bytes=12 * 2**20),
        cost_estimate=pl.CostEstimate(
            flops=4 * 128 * 512 * 2048, bytes_accessed=5 * 2**20, transcendentals=0
        ),
        name="project_far",
    )(own, other, features)


def project_near_kernel(own_ref, other_ref, *refs):
    out_refs = refs[-6:]
    for axis in range(2):
        for number, k in enumerate((0, 1, 3)):
            out_refs[3 * axis + number][...] = partial_sums(
                own_ref, other_ref, refs[:2], axis, k
            )


def project_near(own, other, features, ready):
    vmem = pl.BlockSpec(memory_space=pltpu.VMEM)
    return pl.pallas_call(
        project_near_kernel,
        out_shape=[jax.ShapeDtypeStruct((128, 2 * CUT), BF)] * 6,
        in_specs=[vmem] * 4 + [pl.BlockSpec(memory_space=pl.ANY)] * len(ready),
        out_specs=[vmem] * 6,
        compiler_params=pltpu.CompilerParams(vmem_limit_bytes=12 * 2**20),
        cost_estimate=pl.CostEstimate(
            flops=12 * 128 * 512 * 2048, bytes_accessed=5 * 2**20, transcendentals=0
        ),
        name="project_near",
    )(own, other, *features, *ready)


def dispatch_kernel(
    residual_ref, gain_ref, slot_ref, weight_ref, *refs
):
    sums, (hidden_ref, out_ref, map_ref) = refs[0:2], refs[2:]
    square = jnp.zeros((32, 1), F32)
    for cut in range(4):
        columns = slice(cut * CUT, (cut + 1) * CUT)
        half = slice(cut % 2 * CUT, (cut % 2 + 1) * CUT)
        projected = sums[cut // 2][:, half]
        hidden = projected + residual_ref[:, :, columns].reshape(32, CUT).astype(F32)
        hidden_ref[cut * 32 : (cut + 1) * 32, :] = hidden
        square = square + jnp.sum(hidden * hidden, axis=-1, keepdims=True)
    factor = lax.rsqrt(square / (4 * CUT) + EPSILON)
    normed = jnp.concatenate(
        [
            (
                hidden_ref[cut * 32 : (cut + 1) * 32, :]
                * factor
                * gain_ref[:, cut * CUT : (cut + 1) * CUT]
            ).astype(BF)
            for cut in range(4)
        ],
        axis=0,
    )
    for first in range(0, 2048, 256):
        target = first + lax.broadcasted_iota(jnp.int32, (256, 128), 0)
        hits = jnp.zeros((256, 128), F32)
        value = jnp.zeros((256, 128), F32)
        for choice in range(8):
            hit = target == slot_ref[choice : choice + 1, :]
            hits = jnp.where(hit, 1.0, hits)
            value = jnp.where(hit, weight_ref[choice : choice + 1, :], value)
        out_ref[first : first + 256, :] = jnp.dot(
            hits.astype(BF), normed, preferred_element_type=F32
        ).astype(BF)
        value = value.T
        coarse = value.astype(BF)
        map_ref[0:128, first : first + 256] = coarse
        map_ref[128:256, first : first + 256] = (value - coarse.astype(F32)).astype(BF)


def dispatch(residual, gain, slots, weights, sums):
    vmem = pl.BlockSpec(memory_space=pltpu.VMEM)
    return pl.pallas_call(
        dispatch_kernel,
        out_shape=[
            jax.ShapeDtypeStruct((128, CUT), F32),
            jax.ShapeDtypeStruct((2048, CUT), BF),
            jax.ShapeDtypeStruct((256, 2048), BF),
        ],
        in_specs=[vmem] * 6,
        out_specs=[vmem] * 3,
        compiler_params=pltpu.CompilerParams(vmem_limit_bytes=32 * 2**20),
        cost_estimate=pl.CostEstimate(
            flops=2 * 2048 * 128 * 1024, bytes_accessed=6 * 2**20, transcendentals=32
        ),
        name="dispatch",
    )(residual, gain, slots, weights, *sums)


def combine_kernel(map_ref, returned_ref, hidden_ref, out_ref, held_ref, arrived, *, parts):
    block = 2048 // parts
    copies = []
    for part in range(parts):
        rows = pl.ds(part * block, block)
        copy = pltpu.make_async_copy(returned_ref.at[rows], held_ref.at[rows], arrived.at[part])
        copy.start()
        copies.append(copy)
    total = jnp.zeros((256, CUT), F32)
    for part, copy in enumerate(copies):
        copy.wait()
        rows = slice(part * block, (part + 1) * block)
        total = total + jnp.dot(map_ref[:, rows], held_ref[rows, :], preferred_element_type=F32)
    total = hidden_ref[...] + total[0:128] + total[128:256]
    for cut in range(4):
        out_ref[:, :, cut * CUT : (cut + 1) * CUT] = (
            total[cut * 32 : (cut + 1) * 32].astype(BF).reshape(2, 16, CUT)
        )


def combine(gather, returned, hidden):
    parts = 4
    vmem = pl.BlockSpec(memory_space=pltpu.VMEM)
    return pl.pallas_call(
        functools.partial(combine_kernel, parts=parts),
        out_shape=jax.ShapeDtypeStruct((2, 16, 4 * CUT), BF),
        in_specs=[vmem, pl.BlockSpec(memory_space=pltpu.HBM), vmem],
        out_specs=vmem,
        scratch_shapes=[pltpu.VMEM((2048, CUT), BF), pltpu.SemaphoreType.DMA((parts,))],
        compiler_params=pltpu.CompilerParams(vmem_limit_bytes=32 * 2**20),
        cost_estimate=pl.CostEstimate(
            flops=2 * 256 * 2048 * 1024, bytes_accessed=6 * 2**20, transcendentals=0
        ),
        name="combine",
    )(gather, returned, hidden)


def expert_kernel(
    in_ref, gate_up_hbm, down_hbm, out_ref, w_ref, d_ref, x_ref, act_ref, y_ref, arrived
):
    width = w_ref.shape[3]

    def weights(part):
        return [
            pltpu.make_async_copy(
                gate_up_hbm.at[:, pl.ds(side * 3 * width + part * width, width)],
                w_ref.at[part, side],
                arrived.at[part * 2 + side],
            )
            for side in range(2)
        ]

    def down(cut):
        return pltpu.make_async_copy(
            down_hbm.at[:, pl.ds(cut * CUT, CUT)], d_ref.at[cut], arrived.at[6 + cut]
        )

    coming = weights(0)
    for copy in coming:
        copy.start()
    near = lax.broadcasted_iota(jnp.int32, (128, 128), 0)
    far = lax.broadcasted_iota(jnp.int32, (128, 128), 1)
    to_rows = (near % 32 // 4 * 16 + near // 32 * 4 + near % 4 == far).astype(BF)
    to_blocks = (near % 16 // 4 * 32 + near // 16 * 4 + near % 4 == far).astype(BF)
    for group in range(16):
        mixed = jnp.dot(
            to_rows, in_ref[group * 128 : (group + 1) * 128, :], preferred_element_type=F32
        ).astype(BF)
        for cut in range(4):
            x_ref[group * 32 : (group + 1) * 32, cut * CUT : (cut + 1) * CUT] = mixed[
                cut * 32 : (cut + 1) * 32
            ]
    for part in range(3):
        for copy in coming:
            copy.wait()
        coming = weights(part + 1) if part < 2 else [down(cut) for cut in range(4)]
        for copy in coming:
            copy.start()
        for first in range(0, 512, 256):
            rows = slice(first, first + 256)
            gate = jnp.dot(x_ref[rows], w_ref[part, 0], preferred_element_type=F32)
            up = jnp.dot(x_ref[rows], w_ref[part, 1], preferred_element_type=F32)
            act_ref[rows, part * width : (part + 1) * width] = (
                gate / (1.0 + jnp.exp(-gate)) * up
            ).astype(BF)
    for copy in coming:
        copy.wait()
    for half in range(2):
        rows = slice(half * 256, (half + 1) * 256)
        for cut in range(4):
            y_ref[cut] = jnp.dot(act_ref[rows], d_ref[cut], preferred_element_type=F32).astype(BF)
        for group in range(8):
            together = y_ref[:, group * 32 : (group + 1) * 32, :].reshape(128, CUT)
            first = half * 1024 + group * 128
            out_ref[first : first + 128, :] = jnp.dot(
                to_blocks, together, preferred_element_type=F32
            ).astype(BF)


def run_expert(arrived, gate_up, down_weight):
    width = gate_up.shape[1] // 6
    hbm = pl.BlockSpec(memory_space=pltpu.HBM)
    vmem = pl.BlockSpec(memory_space=pltpu.VMEM)
    return pl.pallas_call(
        expert_kernel,
        out_shape=jax.ShapeDtypeStruct(arrived.shape, BF),
        in_specs=[vmem, hbm, hbm],
        out_specs=vmem,
        scratch_shapes=[
            pltpu.VMEM((3, 2, 4 * CUT, width), BF),
            pltpu.VMEM((4, 3 * width, CUT), BF),
            pltpu.VMEM((512, 4 * CUT), BF),
            pltpu.VMEM((512, 3 * width), BF),
            pltpu.VMEM((4, 256, CUT), BF),
            pltpu.SemaphoreType.DMA((10,)),
        ],
        compiler_params=pltpu.CompilerParams(vmem_limit_bytes=EXPERT_VMEM * 2**20),
        cost_estimate=pl.CostEstimate(
            flops=2 * 512 * 4096 * 768 * 3, bytes_accessed=27 * 2**20, transcendentals=512 * 768
        ),
        name="expert",
    )(arrived, gate_up, down_weight)


def on_device(
    prompt_cache,
    queries,
    new_kv,
    residual,
    out_weight,
    norm_gain,
    gate_up,
    down_weight,
    expert_ids,
    route_weights,
):
    z, y, core = place()
    position = jnp.stack([z, y, core]).astype(jnp.int32)
    everyone = ("sample", "prompt")
    other_weight = to_other_core(out_weight)

    ids = expert_ids.reshape(2, 128)
    ids = ids % 32 * 4 + ids // 32
    row_of = jnp.arange(128, dtype=jnp.int32) // 8
    same = (ids[:, :, None] == ids[:, None, :]) & (row_of[None, :] < row_of[:, None])[None]
    rank = jnp.sum(same.astype(jnp.int32), axis=-1)
    slots = ids * 16 + jnp.arange(2, dtype=jnp.int32)[:, None] * 2 + rank
    slots = slots.reshape(1, 32, 8) + 4 * jnp.arange(4, dtype=jnp.int32)[:, None, None]
    slots = slots.reshape(128, 8)
    weights = jnp.broadcast_to(route_weights.reshape(1, 32, 8), (4, 32, 8)).reshape(128, 8)

    sent = pack(queries, new_kv, prompt_cache[0])
    groups = [
        [2 * (z_at * RING + y_at) + which for y_at in range(RING) for z_at in range(RING)]
        for which in range(2)
    ]
    own = lax.all_to_all(
        sent, "sample", split_axis=0, concat_axis=0, tiled=True, axis_index_groups=groups
    )
    other = to_other_core(own[:, 48:, :])
    features = attend(position, own, other)
    *far, token = project_far(out_weight, other_weight, features)
    steps = (("y", 1), ("y", -1), ("z", 1), ("z", -1))
    passed = [shift_to(part, *step) for part, step in zip(far, steps)]
    rest = attend(position, own, other, token)
    near = project_near(out_weight, other_weight, [features, rest], passed)
    sum_y, sum_z = ring_sums([("y", near[:3], passed[:2]), ("z", near[3:], passed[2:])])
    sums = halving_sums(
        [
            ("z", z, sum_y.reshape(RING, 32, 2 * CUT)),
            ("y", y, sum_z.reshape(RING, 32, 2 * CUT)),
        ]
    )

    hidden, outgoing, gather = dispatch(
        residual, norm_gain.reshape(1, -1), slots.T, weights.T, sums
    )
    arrived = lax.all_to_all(
        outgoing.reshape(128, 16, CUT), everyone, split_axis=0, concat_axis=0, tiled=True
    )
    produced = run_expert(arrived.reshape(2048, CUT), gate_up[0], down_weight[0])
    returned = lax.all_to_all(
        produced.reshape(128, 16, CUT), everyone, split_axis=0, concat_axis=0, tiled=True
    )
    return combine(gather, returned.reshape(2048, CUT), hidden)


def solution(mesh):
    in_specs = (
        P("prompt", "sample", None),
        P(None, ("prompt", "sample"), None),
        P(None, ("prompt", "sample"), None),
        P(None, ("prompt", "sample"), None),
        P("sample", None),
        P(),
        P(("prompt", "sample"), None, None),
        P(("prompt", "sample"), None, None),
        P(None, ("prompt", "sample"), None),
        P(None, ("prompt", "sample"), None),
    )
    out_specs = P(None, ("prompt", "sample"), None)
    return jax.shard_map(
        on_device, mesh=mesh, in_specs=in_specs, out_specs=out_specs, check_vma=False
    )
```
